32 devices in a mesh: row: 8 (over y, x, core), col: 4 (over z).
Axes of the slice: x: 2, y: 2, z: 4, core: 2. Of those that a mesh axis runs over, the one named last changes fastest.
Arguments:
- tile_values: bfloat16 [3072, 256, 256], P(('row', 'col')), may hold values from -0.375 to 0.375
- tile_coords: int32 [3072, 2], P(('row', 'col')), may hold values from 0 to 15, as said below
- live_counts: int32 [32], P(('row', 'col')), may hold values from 24 to 96, as said below
Outputs:
- range_basis: float32 [32768, 192], P(('row', 'col'))
- projected: float32 [4, 4096, 192], P('col', 'row')
The draws below stay inside these ranges and needn't reach their ends.
Inputs may be any that keep to these rules, and one draw needn't show every extreme that they name: `tile_coords`: for each device, column 0 is below 16, column 1 is below 16, and the 96 positions of its slots are distinct. `live_counts`: some device has all 96 slots live.
All inputs are finite; a program needn't handle non-finite values.
Results may differ from the reference program's by a relative error of at most 0.0003.
Values sent between devices are 32-bit elements; how exact they have to be, the bound alone decides.
A program may use at most 128 MiB of HBM per device.

```python
import math
import jax
import jax.numpy as jnp
from jax import lax

TB = 256
K = 192
RT = 16
CT = 16
NT = 96
M = 32768
N_ROW = 8
N_COL = 4


def draw_tile_values(key, part):
    device_total = N_ROW * N_COL
    base_key = jax.random.fold_in(key, 11)

    def device_draw(device_id):
        device_key = jax.random.fold_in(base_key, device_id)
        block = jnp.clip(0.125 + 0.0625 * jax.random.normal(device_key, (NT, TB, TB), jnp.float32), -0.375, 0.375)
        return block.astype(jnp.bfloat16)
    drawn = lax.map(device_draw, jnp.arange(device_total, dtype=jnp.int32))
    return drawn.reshape(device_total * NT, TB, TB)


def draw_tile_coords(key, part):
    device_total = N_ROW * N_COL
    device_keys = jax.random.split(key, device_total)

    def device_draw(device_key):
        ordering = jax.random.permutation(device_key, RT * CT)[:NT].astype(jnp.int32)
        return jnp.stack([ordering // CT, ordering % CT], axis=1).astype(jnp.int32)
    return jax.vmap(device_draw)(device_keys).reshape(device_total * NT, 2)


def draw_live_counts(key, part):
    device_total = N_ROW * N_COL
    counts_drawn = jax.random.randint(key, (device_total,), max(1, NT // 4), NT + 1, dtype=jnp.int32)
    chosen = jax.random.randint(jax.random.fold_in(key, 7), (), 0, device_total, dtype=jnp.int32)
    return counts_drawn.at[chosen].set(NT)


def setup_inputs(seed: int = 0) -> dict:
    key_of = jax.random.split(jax.random.key(seed), 4)
    tile_values = draw_tile_values(jax.random.fold_in(key_of[3], 71), 0)
    tile_coords = draw_tile_coords(jax.random.fold_in(key_of[3], 71), 0)
    live_counts = draw_live_counts(jax.random.fold_in(key_of[3], 71), 0)
    return {"tile_values": tile_values, "tile_coords": tile_coords, "live_counts": live_counts}


def sketch_signs(column_ids, rank_cols):
    rank_index = jnp.arange(rank_cols, dtype=jnp.int32)
    hashed = column_ids[..., None] * rank_cols + rank_index
    hashed = hashed * 747796405 + 1442695040
    hashed = hashed ^ hashed >> 15
    hashed = hashed * 1103515245 + 12345
    hashed = hashed ^ hashed >> 13
    return (1 - 2 * (hashed >> 9 & 1)).astype(jnp.float32)

def reference(tile_values, tile_coords, live_counts):
    device_total = N_ROW * N_COL
    values = tile_values.reshape(device_total, NT, TB, TB)
    coords = tile_coords.reshape(device_total, NT, 2)
    device_ids = jnp.arange(device_total, dtype=jnp.int32)
    slot_ids = jnp.arange(NT, dtype=jnp.int32)

    def sketch_step(running, inputs):
        tile_block, slot_coords, live_total, device_id = inputs
        row_dev = device_id // N_COL
        col_dev = device_id % N_COL
        live_mask = (slot_ids < live_total).astype(jnp.float32)[:, None, None]
        column_ids = col_dev * (CT * TB) + slot_coords[:, 1:2] * TB + jnp.arange(TB, dtype=jnp.int32)[None, :]
        test_signs = sketch_signs(column_ids, K)
        tile_terms = jnp.einsum('tij,tjk->tik', tile_block.astype(jnp.float32), test_signs, precision=lax.Precision.HIGHEST) * live_mask
        row_ids = row_dev * RT + slot_coords[:, 0]
        return (running.at[row_ids].add(tile_terms), None)
    start = jnp.zeros((RT * N_ROW, TB, K), jnp.float32)
    sketch, _ = lax.scan(sketch_step, start, (values, coords, live_counts, device_ids))
    sketch = sketch.reshape(M, K)
    gram_matrix = jnp.dot(sketch.T.astype(jnp.float32), sketch.astype(jnp.float32), precision=lax.Precision.HIGHEST, preferred_element_type=jnp.float32)
    factor = jnp.linalg.cholesky(gram_matrix)
    solved = jax.scipy.linalg.solve_triangular(factor, sketch.T, lower=True)
    range_basis = math.sqrt(M) * solved.T
    basis_blocks = range_basis.reshape(RT * N_ROW, TB, K)

    def adjoint_step(running, inputs):
        tile_block, slot_coords, live_total, device_id = inputs
        row_dev = device_id // N_COL
        col_dev = device_id % N_COL
        live_mask = (slot_ids < live_total).astype(jnp.float32)[:, None, None]
        picked = basis_blocks[row_dev * RT + slot_coords[:, 0]]
        tile_terms = jnp.einsum('tij,tik->tjk', tile_block.astype(jnp.float32), picked, precision=lax.Precision.HIGHEST) * live_mask
        col_ids = col_dev * CT + slot_coords[:, 1]
        return (running.at[col_ids].add(tile_terms), None)
    begin = jnp.zeros((CT * N_COL, TB, K), jnp.float32)
    projected, _ = lax.scan(adjoint_step, begin, (values, coords, live_counts, device_ids))
    return (range_basis, projected.reshape(N_COL, CT * TB, K))
```

```python
import functools
import math

import jax
import jax.numpy as jnp
from jax import lax
from jax.experimental import pallas as pl
from jax.experimental.pallas import tpu as pltpu
from jax.sharding import PartitionSpec as P

K = 192
RT = 16
CT = 16
CHUNKS = 12
HIGHEST = lax.Precision.HIGHEST


def load_tiles(tiles_hbm, tiles, sems):
    per = tiles.shape[0] // CHUNKS
    return [
        pltpu.make_async_copy(
            tiles_hbm.at[pl.ds(c * per, per)], tiles.at[pl.ds(c * per, per)], sems.at[c]
        )
        for c in range(CHUNKS)
    ]


def sketch_kernel(coords, live, base, tiles_hbm, out, tiles, signs, sems):
    tb = tiles.shape[1]
    copies = load_tiles(tiles_hbm, tiles, sems)
    for copy in copies:
        copy.start()
    out[...] = jnp.zeros_like(out)

    def make_signs(j, carry):
        column = lax.broadcasted_iota(jnp.int32, (K, tb), 1) + (base[0] + j * tb)
        h = column * K + lax.broadcasted_iota(jnp.int32, (K, tb), 0)
        h = h * 747796405 + 1442695040
        h = h ^ (h >> 15)
        h = h * 1103515245 + 12345
        h = h ^ (h >> 13)
        signs[j] = (1 - 2 * ((h >> 9) & 1)).astype(jnp.float32).astype(jnp.bfloat16)
        return carry

    lax.fori_loop(0, CT, make_signs, 0)
    per = tiles.shape[0] // CHUNKS
    for c, copy in enumerate(copies):
        copy.wait()

        def step(s, carry):
            i = coords[s, 0]
            j = coords[s, 1]
            out[i] += lax.dot_general(
                signs[j], tiles[s], (((1,), (1,)), ((), ())), preferred_element_type=jnp.float32
            )
            return carry

        lax.fori_loop(c * per, jnp.minimum((c + 1) * per, live[0]), step, 0)


def adjoint_kernel(coords, live, tiles_hbm, sketch_hbm, out, tiles, sketch, parts, sems, sketch_sem):
    half = out.shape[2]
    sketch_copy = pltpu.make_async_copy(sketch_hbm, sketch, sketch_sem)
    sketch_copy.start()
    copies = load_tiles(tiles_hbm, tiles, sems)
    for copy in copies:
        copy.start()
    out[...] = jnp.zeros_like(out)
    sketch_copy.wait()

    def split(i, carry):
        x = sketch[i]
        for p in range(3):
            y = x.astype(jnp.bfloat16)
            parts[i, p * K : (p + 1) * K, :] = y
            x = x - y.astype(jnp.float32)
        return carry

    lax.fori_loop(0, RT, split, 0)
    per = tiles.shape[0] // CHUNKS
    for c, copy in enumerate(copies):
        copy.wait()

        def step(s, carry):
            i = coords[s, 0]
            j = coords[s, 1]
            t = jnp.dot(parts[i], tiles[s], preferred_element_type=jnp.float32)
            t = t[:K] + t[K : 2 * K] + t[2 * K :]
            out[2 * j] += t[:, :half]
            out[2 * j + 1] += t[:, half:]
            return carry

        lax.fori_loop(c * per, jnp.minimum((c + 1) * per, live[0]), step, 0)


SMEM = pl.BlockSpec(memory_space=pltpu.SMEM)
VMEM = pl.BlockSpec(memory_space=pltpu.VMEM)
ANY = pl.BlockSpec(memory_space=pl.ANY)


def sketch_call(tile_coords, live_counts, base, tile_values):
    slots, tb, _ = tile_values.shape
    return pl.pallas_call(
        sketch_kernel,
        out_shape=jax.ShapeDtypeStruct((RT, K, tb), jnp.float32),
        in_specs=[SMEM, SMEM, SMEM, ANY],
        out_specs=VMEM,
        scratch_shapes=[
            pltpu.VMEM((slots, tb, tb), jnp.bfloat16),
            pltpu.VMEM((CT, K, tb), jnp.bfloat16),
            pltpu.SemaphoreType.DMA((CHUNKS,)),
        ],
        compiler_params=pltpu.CompilerParams(vmem_limit_bytes=40 << 20),
        cost_estimate=pl.CostEstimate(
            flops=2 * slots * tb * tb * K, bytes_accessed=slots * tb * tb * 2, transcendentals=0
        ),
    )(tile_coords, live_counts, base, tile_values)


def adjoint_call(tile_coords, live_counts, tile_values, sketch_t):
    slots, tb, _ = tile_values.shape
    return pl.pallas_call(
        adjoint_kernel,
        out_shape=jax.ShapeDtypeStruct((2 * CT, K, tb // 2), jnp.float32),
        in_specs=[SMEM, SMEM, ANY, ANY],
        out_specs=VMEM,
        scratch_shapes=[
            pltpu.VMEM((slots, tb, tb), jnp.bfloat16),
            pltpu.VMEM((RT, K, tb), jnp.float32),
            pltpu.VMEM((RT, 3 * K, tb), jnp.bfloat16),
            pltpu.SemaphoreType.DMA((CHUNKS,)),
            pltpu.SemaphoreType.DMA,
        ],
        compiler_params=pltpu.CompilerParams(vmem_limit_bytes=48 << 20),
        cost_estimate=pl.CostEstimate(
            flops=6 * slots * tb * tb * K, bytes_accessed=slots * tb * tb * 2, transcendentals=0
        ),
    )(tile_coords, live_counts, tile_values, sketch_t)


def per_device(tile_values, tile_coords, live_counts):
    tb = tile_values.shape[1]
    base = (lax.axis_index("col") * (CT * tb)).reshape(1)
    scale = math.sqrt(RT * tb * lax.axis_size("row"))
    part = sketch_call(tile_coords, live_counts, base, tile_values)
    share = lax.psum_scatter(part, "col", scatter_dimension=0, tiled=True)
    full = lax.all_gather(share, "col", axis=0, tiled=True)
    gram = jnp.einsum(
        "bkn,bln->kl", share, share, precision=HIGHEST, preferred_element_type=jnp.float32
    )
    gram = lax.psum(gram, ("row", "col"))
    factor = jnp.linalg.cholesky(gram)
    inverse = scale * jax.scipy.linalg.solve_triangular(
        factor, jnp.eye(K, dtype=jnp.float32), lower=True
    )
    basis = jnp.einsum("bkn,lk->bnl", share, inverse, precision=HIGHEST).reshape(-1, K)
    adjoint = adjoint_call(tile_coords, live_counts, tile_values, full)
    mine = lax.psum_scatter(adjoint, "row", scatter_dimension=0, tiled=True)
    projected = jnp.einsum("bkn,lk->bnl", mine, inverse, precision=HIGHEST).reshape(1, -1, K)
    return basis, projected


def solution(mesh):
    in_specs = (P(("row", "col"), None, None), P(("row", "col"), None), P(("row", "col")))
    out_specs = (P(("row", "col"), None), P("col", "row", None))
    return jax.shard_map(
        per_device, mesh=mesh, in_specs=in_specs, out_specs=out_specs, check_vma=False
    )
```

```python
import functools
import math

import jax
import jax.numpy as jnp
from jax import lax
from jax.experimental import pallas as pl
from jax.experimental.pallas import tpu as pltpu
from jax.sharding import PartitionSpec as P

K = 192
RT = 16
CT = 16
CHUNKS = 12
HIGHEST = lax.Precision.HIGHEST


def load_tiles(tiles_hbm, tiles, sems):
    per = tiles.shape[0] // CHUNKS
    return [
        pltpu.make_async_copy(
            tiles_hbm.at[pl.ds(c * per, per)], tiles.at[pl.ds(c * per, per)], sems.at[c]
        )
        for c in range(CHUNKS)
    ]


def sketch_kernel(coords, live, base, tiles_hbm, out, tiles, signs, sems):
    tb = tiles.shape[1]
    half = tb // 2
    copies = load_tiles(tiles_hbm, tiles, sems)
    for copy in copies:
        copy.start()
    out[...] = jnp.zeros_like(out)

    def make_signs(j, carry):
        column = lax.broadcasted_iota(jnp.int32, (K, tb), 1) + (base[0] + j * tb)
        h = column * K + lax.broadcasted_iota(jnp.int32, (K, tb), 0)
        h = h * 747796405 + 1442695040
        h = h ^ (h >> 15)
        h = h * 1103515245 + 12345
        h = h ^ (h >> 13)
        signs[j] = (1 - 2 * ((h >> 9) & 1)).astype(jnp.float32).astype(jnp.bfloat16)
        return carry

    lax.fori_loop(0, CT, make_signs, 0)
    per = tiles.shape[0] // CHUNKS
    for c, copy in enumerate(copies):
        copy.wait()

        def step(s, carry):
            i = coords[s, 0]
            j = coords[s, 1]
            t = lax.dot_general(
                signs[j], tiles[s], (((1,), (1,)), ((), ())), preferred_element_type=jnp.float32
            )
            out[2 * i] += t[:, :half]
            out[2 * i + 1] += t[:, half:]
            return carry

        lax.fori_loop(c * per, jnp.minimum((c + 1) * per, live[0]), step, 0)


def adjoint_kernel(coords, live, tiles_hbm, sketch_hbm, out, tiles, sketch, parts, sems, sketch_sem):
    half = out.shape[2]
    sketch_copy = pltpu.make_async_copy(sketch_hbm, sketch, sketch_sem)
    sketch_copy.start()
    copies = load_tiles(tiles_hbm, tiles, sems)
    for copy in copies:
        copy.start()
    out[...] = jnp.zeros_like(out)
    sketch_copy.wait()

    def split(i, carry):
        x = jnp.concatenate([sketch[2 * i], sketch[2 * i + 1]], axis=1)
        for p in range(3):
            y = x.astype(jnp.bfloat16)
            parts[i, p * K : (p + 1) * K, :] = y
            x = x - y.astype(jnp.float32)
        return carry

    lax.fori_loop(0, RT, split, 0)
    per = tiles.shape[0] // CHUNKS
    for c, copy in enumerate(copies):
        copy.wait()

        def step(s, carry):
            i = coords[s, 0]
            j = coords[s, 1]
            t = jnp.dot(parts[i], tiles[s], preferred_element_type=jnp.float32)
            t = t[:K] + t[K : 2 * K] + t[2 * K :]
            out[2 * j] += t[:, :half]
            out[2 * j + 1] += t[:, half:]
            return carry

        lax.fori_loop(c * per, jnp.minimum((c + 1) * per, live[0]), step, 0)


MESH = pl.DeviceIdType.MESH
SMEM = pl.BlockSpec(memory_space=pltpu.SMEM)
VMEM = pl.BlockSpec(memory_space=pltpu.VMEM)
ANY = pl.BlockSpec(memory_space=pl.ANY)


def sketch_call(tile_coords, live_counts, base, tile_values):
    slots, tb, _ = tile_values.shape
    return pl.pallas_call(
        sketch_kernel,
        out_shape=jax.ShapeDtypeStruct((2 * RT, K, tb // 2), jnp.float32),
        in_specs=[SMEM, SMEM, SMEM, ANY],
        out_specs=VMEM,
        scratch_shapes=[
            pltpu.VMEM((slots, tb, tb), jnp.bfloat16),
            pltpu.VMEM((CT, K, tb), jnp.bfloat16),
            pltpu.SemaphoreType.DMA((CHUNKS,)),
        ],
        compiler_params=pltpu.CompilerParams(vmem_limit_bytes=40 << 20),
        cost_estimate=pl.CostEstimate(
            flops=2 * slots * tb * tb * K, bytes_accessed=slots * tb * tb * 2, transcendentals=0
        ),
    )(tile_coords, live_counts, base, tile_values)


def adjoint_call(tile_coords, live_counts, tile_values, sketch_t):
    slots, tb, _ = tile_values.shape
    return pl.pallas_call(
        adjoint_kernel,
        out_shape=jax.ShapeDtypeStruct((2 * CT, K, tb // 2), jnp.float32),
        in_specs=[SMEM, SMEM, ANY, ANY],
        out_specs=VMEM,
        scratch_shapes=[
            pltpu.VMEM((slots, tb, tb), jnp.bfloat16),
            pltpu.VMEM((2 * RT, K, tb // 2), jnp.float32),
            pltpu.VMEM((RT, 3 * K, tb), jnp.bfloat16),
            pltpu.SemaphoreType.DMA((CHUNKS,)),
            pltpu.SemaphoreType.DMA,
        ],
        compiler_params=pltpu.CompilerParams(vmem_limit_bytes=48 << 20),
        cost_estimate=pl.CostEstimate(
            flops=6 * slots * tb * tb * K, bytes_accessed=slots * tb * tb * 2, transcendentals=0
        ),
    )(tile_coords, live_counts, tile_values, sketch_t)


def partner_of(index, bit):
    step = 1 << bit
    return index + step * (1 - 2 * ((index // step) % 2))


def greet(n_col, bits):
    barrier = pltpu.get_barrier_semaphore()
    col = lax.axis_index("col")
    row = lax.axis_index("row")
    expected = bits
    for bit in range(bits):
        pl.semaphore_signal(barrier, inc=1, device_id={"row": partner_of(row, bit)}, device_id_type=MESH)
    if n_col:

        @pl.when(col > 0)
        def _():
            pl.semaphore_signal(barrier, inc=1, device_id={"col": col - 1}, device_id_type=MESH)

        @pl.when(col < n_col - 1)
        def _():
            pl.semaphore_signal(barrier, inc=1, device_id={"col": col + 1}, device_id_type=MESH)

        expected = bits + jnp.where(col > 0, 1, 0) + jnp.where(col < n_col - 1, 1, 0)
    pl.semaphore_wait(barrier, expected)


def line_kernel(
    n_col, bits, part, out, gram, inbox, grams, gram_in, s_red, r_red, s_cast, r_cast, s_gram, r_gram
):
    col = lax.axis_index("col")
    row = lax.axis_index("row")
    count = part.shape[0] // 2
    lag = n_col
    greet(n_col, bits)
    first = (col == 0, col == n_col - 1)
    ends = (first[0], first[1])
    starts = (first[1], first[0])
    towards = (col - 1, col + 1)
    away = (col + 1, col - 1)

    def reduce_copy(flow, q, src):
        return pltpu.make_async_remote_copy(
            src_ref=src.at[flow * count + q],
            dst_ref=inbox.at[flow * count + q],
            send_sem=s_red.at[flow, q],
            recv_sem=r_red.at[flow, q],
            device_id={"col": towards[flow]},
            device_id_type=MESH,
        )

    def cast_copy(flow, q):
        return pltpu.make_async_remote_copy(
            src_ref=out.at[flow * count + q],
            dst_ref=out.at[flow * count + q],
            send_sem=s_cast.at[flow, q],
            recv_sem=r_cast.at[flow, q],
            device_id={"col": away[flow]},
            device_id_type=MESH,
        )

    grams[0] = jnp.zeros_like(grams[0])

    def step(q, carry):
        @pl.when(q < count)
        def _():
            for flow in range(2):
                b = flow * count + q

                @pl.when(starts[flow])
                def _():
                    reduce_copy(flow, q, part).start()

                @pl.when(jnp.logical_not(starts[flow]))
                def _():
                    reduce_copy(flow, q, part).wait_recv()

                    @pl.when(ends[flow])
                    def _():
                        out[b] = part[b] + inbox[b]
                        cast_copy(flow, q).start()

                    @pl.when(jnp.logical_not(ends[flow]))
                    def _():
                        inbox[b] = part[b] + inbox[b]
                        reduce_copy(flow, q, inbox).start()

        @pl.when(q >= lag)
        def _():
            p = q - lag
            for flow in range(2):

                @pl.when(jnp.logical_not(ends[flow]))
                def _():
                    cast_copy(flow, p).wait_recv()

                    @pl.when(jnp.logical_not(starts[flow]))
                    def _():
                        cast_copy(flow, p).start()

            for flow in range(2):
                x = out[flow * count + p]
                grams[0] += lax.dot_general(
                    x, x, (((1,), (1,)), ((), ())), precision=HIGHEST, preferred_element_type=jnp.float32
                )

        return carry

    lax.fori_loop(0, count + lag, step, 0)
    for bit in range(bits):
        copy = pltpu.make_async_remote_copy(
            src_ref=grams.at[bit],
            dst_ref=gram_in.at[bit],
            send_sem=s_gram.at[bit],
            recv_sem=r_gram.at[bit],
            device_id={"row": partner_of(row, bit)},
            device_id_type=MESH,
        )
        copy.start()
        copy.wait()
        grams[bit + 1] = grams[bit] + gram_in[bit]
    gram[...] = grams[bits]

    def drain(q, carry):
        for flow in range(2):

            @pl.when(jnp.logical_not(ends[flow]))
            def _():
                reduce_copy(flow, q, part).wait_send()

            @pl.when(jnp.logical_not(starts[flow]))
            def _():
                cast_copy(flow, q).wait_send()

        return carry

    lax.fori_loop(0, count, drain, 0)


def line_call(n_col, bits, part):
    blocks = part.shape[0]
    dma = pltpu.SemaphoreType.DMA
    return pl.pallas_call(
        functools.partial(line_kernel, n_col, bits),
        out_shape=(
            jax.ShapeDtypeStruct(part.shape, jnp.float32),
            jax.ShapeDtypeStruct((K, K), jnp.float32),
        ),
        in_specs=[VMEM],
        out_specs=(VMEM, VMEM),
        scratch_shapes=[
            pltpu.VMEM(part.shape, jnp.float32),
            pltpu.VMEM((bits + 1, K, K), jnp.float32),
            pltpu.VMEM((bits, K, K), jnp.float32),
            dma((2, blocks // 2)),
            dma((2, blocks // 2)),
            dma((2, blocks // 2)),
            dma((2, blocks // 2)),
            dma((bits,)),
            dma((bits,)),
        ],
        compiler_params=pltpu.CompilerParams(
            collective_id=0, has_side_effects=True, vmem_limit_bytes=32 << 20
        ),
    )(part)


def halving_kernel(bits, part, out, *scratch):
    inboxes, s_sem, r_sem = scratch[:bits], scratch[bits], scratch[bits + 1]
    row = lax.axis_index("row")
    n_row = 1 << bits
    per = part.shape[0] // n_row
    kh = K // 2
    greet(0, bits)
    orders = (list(range(bits)), [0] + list(range(bits - 1, 0, -1)))

    def bit_of(index, bit):
        return (index // (1 << bit)) % 2

    def at(level, stream, mine, e):
        order = orders[stream]
        value = bit_of(row, order[level])
        value = value if mine else 1 - value
        rest = bits - 1 - level
        if level:
            return inboxes[level - 1].at[stream, value * (1 << rest) + e]
        dest = value * (1 << order[0])
        for i in range(rest):
            dest = dest + ((e >> (rest - 1 - i)) & 1) * (1 << order[1 + i])
        return part.at[pl.ds(dest * per, per), pl.ds(stream * kh, kh)]

    def copy_of(level, stream, e):
        base = sum(1 << (bits - 1 - l) for l in range(level))
        return pltpu.make_async_remote_copy(
            src_ref=at(level, stream, False, e),
            dst_ref=inboxes[level].at[stream, e],
            send_sem=s_sem.at[stream, base + e],
            recv_sem=r_sem.at[stream, base + e],
            device_id={"row": partner_of(row, orders[stream][level])},
            device_id_type=MESH,
        )

    sent = []
    for level in range(bits):
        slots = range(1 << (bits - 1 - level))
        copies = [(e, stream, copy_of(level, stream, e)) for e in slots for stream in range(2)]
        for _, _, copy in copies:
            copy.start()
        for e, stream, copy in copies:
            copy.wait_recv()
            total = inboxes[level][stream, e] + at(level, stream, True, e)[...]
            if level < bits - 1:
                inboxes[level][stream, e] = total
            else:
                out[:, stream * kh : (stream + 1) * kh, :] = total
        sent += copies
    for _, _, copy in sent:
        copy.wait_send()


def halving_call(bits, part):
    blocks, _, lanes = part.shape
    per = blocks >> bits
    dma = pltpu.SemaphoreType.DMA
    return pl.pallas_call(
        functools.partial(halving_kernel, bits),
        out_shape=jax.ShapeDtypeStruct((per, K, lanes), jnp.float32),
        in_specs=[VMEM],
        out_specs=VMEM,
        scratch_shapes=[
            pltpu.VMEM((2, 1 << (bits - 1 - level), per, K // 2, lanes), jnp.float32)
            for level in range(bits)
        ]
        + [dma((2, (1 << bits) - 1)), dma((2, (1 << bits) - 1))],
        compiler_params=pltpu.CompilerParams(
            collective_id=1, has_side_effects=True, vmem_limit_bytes=32 << 20
        ),
    )(part)


def dot_nt(a, b):
    return lax.dot_general(
        a, b, (((1,), (1,)), ((), ())), precision=HIGHEST, preferred_element_type=jnp.float32
    )


def invert_block(d):
    b = d.shape[0]
    rows = lax.broadcasted_iota(jnp.int32, (b, 1), 0)
    eye = (rows == lax.broadcasted_iota(jnp.int32, (b, b), 1)).astype(jnp.float32)
    x = jnp.concatenate([d, eye], axis=1)
    pivots = jnp.zeros((b, 1), jnp.float32)
    for k in range(b):
        row = x[k : k + 1, :]
        pivot = x[k : k + 1, k : k + 1]
        pivots = jnp.where(rows == k, pivot, pivots)
        ratio = jnp.where(rows > k, x[:, k : k + 1] / pivot, 0.0)
        x = x - ratio * row
    return x[:, b:] * lax.rsqrt(pivots)


def factor_kernel(scale, gram, out):
    b = K // 3
    g = gram[...]
    w = scale * (
        lax.broadcasted_iota(jnp.int32, (K, K), 0) == lax.broadcasted_iota(jnp.int32, (K, K), 1)
    ).astype(jnp.float32)
    for p in range(3):
        inverse = invert_block(g[:b, :b])
        top = jnp.dot(inverse, w[:b], precision=HIGHEST, preferred_element_type=jnp.float32)
        out[p * b : (p + 1) * b, :] = top
        if p < 2:
            lower = dot_nt(g[b:, :b], inverse)
            g = g[b:, b:] - dot_nt(lower, lower)
            w = w[b:] - jnp.dot(lower, top, precision=HIGHEST, preferred_element_type=jnp.float32)


def per_device(tile_values, tile_coords, live_counts):
    tb = tile_values.shape[1]
    col = lax.axis_index("col")
    n_col, n_row = lax.axis_size("col"), lax.axis_size("row")
    bits = n_row.bit_length() - 1
    base = (col * (CT * tb)).reshape(1)
    scale = math.sqrt(RT * tb * n_row)
    part = sketch_call(tile_coords, live_counts, base, tile_values)
    full, gram = line_call(n_col, bits, part)
    inverse = pl.pallas_call(
        functools.partial(factor_kernel, scale),
        out_shape=jax.ShapeDtypeStruct((K, K), jnp.float32),
        in_specs=[VMEM],
        out_specs=VMEM,
    )(gram)
    share_blocks = full.shape[0] // n_col
    share = lax.dynamic_slice_in_dim(full, col * share_blocks, share_blocks, 0)
    basis = jnp.einsum("bkn,lk->bnl", share, inverse, precision=HIGHEST).reshape(-1, K)
    adjoint = adjoint_call(tile_coords, live_counts, tile_values, full)
    mine = halving_call(bits, adjoint)
    projected = jnp.einsum("bkn,lk->bnl", mine, inverse, precision=HIGHEST).reshape(1, -1, K)
    return basis, projected


def solution(mesh):
    in_specs = (P(("row", "col"), None, None), P(("row", "col"), None), P(("row", "col")))
    out_specs = (P(("row", "col"), None), P("col", "row", None))
    return jax.shard_map(
        per_device, mesh=mesh, in_specs=in_specs, out_specs=out_specs, check_vma=False
    )
```

```python
import functools
import math

import jax
import jax.numpy as jnp
from jax import lax
from jax.experimental import pallas as pl
from jax.experimental.pallas import tpu as pltpu
from jax.sharding import PartitionSpec as P

K = 192
RT = 16
CT = 16
CHUNKS = 12
LAG = 2
HIGHEST = lax.Precision.HIGHEST


def load_tiles(tiles_hbm, tiles, sems):
    per = tiles.shape[0] // CHUNKS
    return [
        pltpu.make_async_copy(
            tiles_hbm.at[pl.ds(c * per, per)], tiles.at[pl.ds(c * per, per)], sems.at[c]
        )
        for c in range(CHUNKS)
    ]


def sketch_kernel(coords, live, base, tiles_hbm, out, tiles, signs, sems):
    tb = tiles.shape[1]
    half = tb // 2
    copies = load_tiles(tiles_hbm, tiles, sems)
    for copy in copies:
        copy.start()
    out[...] = jnp.zeros_like(out)

    def make_signs(j, carry):
        column = lax.broadcasted_iota(jnp.int32, (K, tb), 1) + (base[0] + j * tb)
        h = column * K + lax.broadcasted_iota(jnp.int32, (K, tb), 0)
        h = h * 747796405 + 1442695040
        h = h ^ (h >> 15)
        h = h * 1103515245 + 12345
        h = h ^ (h >> 13)
        signs[j] = (1 - 2 * ((h >> 9) & 1)).astype(jnp.float32).astype(jnp.bfloat16)
        return carry

    lax.fori_loop(0, CT, make_signs, 0)
    per = tiles.shape[0] // CHUNKS
    for c, copy in enumerate(copies):
        copy.wait()

        def step(s, carry):
            i = coords[s, 0]
            j = coords[s, 1]
            t = lax.dot_general(
                signs[j], tiles[s], (((1,), (1,)), ((), ())), preferred_element_type=jnp.float32
            )
            out[2 * i] += t[:, :half]
            out[2 * i + 1] += t[:, half:]
            return carry

        lax.fori_loop(c * per, jnp.minimum((c + 1) * per, live[0]), step, 0)


def adjoint_kernel(coords, live, tiles_hbm, sketch_hbm, out, tiles, sketch, parts, sems, sketch_sem):
    half = out.shape[2]
    sketch_copy = pltpu.make_async_copy(sketch_hbm, sketch, sketch_sem)
    sketch_copy.start()
    copies = load_tiles(tiles_hbm, tiles, sems)
    for copy in copies:
        copy.start()
    out[...] = jnp.zeros_like(out)
    sketch_copy.wait()

    def split(i, carry):
        x = jnp.concatenate([sketch[2 * i], sketch[2 * i + 1]], axis=1)
        for p in range(3):
            y = x.astype(jnp.bfloat16)
            parts[i, p * K : (p + 1) * K, :] = y
            x = x - y.astype(jnp.float32)
        return carry

    lax.fori_loop(0, RT, split, 0)
    per = tiles.shape[0] // CHUNKS
    for c, copy in enumerate(copies):
        copy.wait()

        def step(s, carry):
            i = coords[s, 0]
            j = coords[s, 1]
            t = jnp.dot(parts[i], tiles[s], preferred_element_type=jnp.float32)
            t = t[:K] + t[K : 2 * K] + t[2 * K :]
            out[2 * j] += t[:, :half]
            out[2 * j + 1] += t[:, half:]
            return carry

        lax.fori_loop(c * per, jnp.minimum((c + 1) * per, live[0]), step, 0)


MESH = pl.DeviceIdType.MESH
SMEM = pl.BlockSpec(memory_space=pltpu.SMEM)
VMEM = pl.BlockSpec(memory_space=pltpu.VMEM)
ANY = pl.BlockSpec(memory_space=pl.ANY)


def sketch_call(tile_coords, live_counts, base, tile_values):
    slots, tb, _ = tile_values.shape
    return pl.pallas_call(
        sketch_kernel,
        out_shape=jax.ShapeDtypeStruct((2 * RT, K, tb // 2), jnp.float32),
        in_specs=[SMEM, SMEM, SMEM, ANY],
        out_specs=VMEM,
        scratch_shapes=[
            pltpu.VMEM((slots, tb, tb), jnp.bfloat16),
            pltpu.VMEM((CT, K, tb), jnp.bfloat16),
            pltpu.SemaphoreType.DMA((CHUNKS,)),
        ],
        compiler_params=pltpu.CompilerParams(vmem_limit_bytes=40 << 20),
        cost_estimate=pl.CostEstimate(
            flops=2 * slots * tb * tb * K, bytes_accessed=slots * tb * tb * 2, transcendentals=0
        ),
    )(tile_coords, live_counts, base, tile_values)


def adjoint_call(tile_coords, live_counts, tile_values, sketch_t):
    slots, tb, _ = tile_values.shape
    return pl.pallas_call(
        adjoint_kernel,
        out_shape=jax.ShapeDtypeStruct((2 * CT, K, tb // 2), jnp.float32),
        in_specs=[SMEM, SMEM, ANY, ANY],
        out_specs=VMEM,
        scratch_shapes=[
            pltpu.VMEM((slots, tb, tb), jnp.bfloat16),
            pltpu.VMEM((2 * RT, K, tb // 2), jnp.float32),
            pltpu.VMEM((RT, 3 * K, tb), jnp.bfloat16),
            pltpu.SemaphoreType.DMA((CHUNKS,)),
            pltpu.SemaphoreType.DMA,
        ],
        compiler_params=pltpu.CompilerParams(vmem_limit_bytes=48 << 20),
        cost_estimate=pl.CostEstimate(
            flops=6 * slots * tb * tb * K, bytes_accessed=slots * tb * tb * 2, transcendentals=0
        ),
    )(tile_coords, live_counts, tile_values, sketch_t)


def partner_of(index, bit):
    step = 1 << bit
    return index + step * (1 - 2 * ((index // step) % 2))


def greet(n_col, bits):
    barrier = pltpu.get_barrier_semaphore()
    col = lax.axis_index("col")
    row = lax.axis_index("row")
    expected = bits
    for bit in range(bits):
        pl.semaphore_signal(barrier, inc=1, device_id={"row": partner_of(row, bit)}, device_id_type=MESH)
    if n_col:

        @pl.when(col > 0)
        def _():
            pl.semaphore_signal(barrier, inc=1, device_id={"col": col - 1}, device_id_type=MESH)

        @pl.when(col < n_col - 1)
        def _():
            pl.semaphore_signal(barrier, inc=1, device_id={"col": col + 1}, device_id_type=MESH)

        expected = bits + jnp.where(col > 0, 1, 0) + jnp.where(col < n_col - 1, 1, 0)
    pl.semaphore_wait(barrier, expected)


def line_kernel(
    n_col, bits, part, out, gram, inbox, grams, gram_in, s_red, r_red, s_cast, r_cast, s_gram, r_gram
):
    col = lax.axis_index("col")
    row = lax.axis_index("row")
    count = part.shape[0] // 2
    greet(n_col, bits)
    first = (col == 0, col == n_col - 1)
    ends = (first[0], first[1])
    starts = (first[1], first[0])
    towards = (col - 1, col + 1)
    away = (col + 1, col - 1)

    def reduce_copy(flow, q, src):
        return pltpu.make_async_remote_copy(
            src_ref=src.at[flow * count + q],
            dst_ref=inbox.at[flow * count + q],
            send_sem=s_red.at[flow, q],
            recv_sem=r_red.at[flow, q],
            device_id={"col": towards[flow]},
            device_id_type=MESH,
        )

    def cast_copy(flow, q):
        return pltpu.make_async_remote_copy(
            src_ref=out.at[flow * count + q],
            dst_ref=out.at[flow * count + q],
            send_sem=s_cast.at[flow, q],
            recv_sem=r_cast.at[flow, q],
            device_id={"col": away[flow]},
            device_id_type=MESH,
        )

    for flow in range(2):

        @pl.when(starts[flow])
        def _():
            def send(q, carry):
                reduce_copy(flow, q, part).start()
                return carry

            lax.fori_loop(0, count, send, 0)

    grams[0] = jnp.zeros_like(grams[0])
    hops = (n_col - 1 - col, col)

    def step(t, carry):
        for flow in range(2):
            q = t - hops[flow] * LAG
            b = flow * count + q

            @pl.when((q >= 0) & (q < count) & jnp.logical_not(starts[flow]))
            def _():
                reduce_copy(flow, q, part).wait_recv()

                @pl.when(ends[flow])
                def _():
                    out[b] = part[b] + inbox[b]
                    cast_copy(flow, q).start()

                @pl.when(jnp.logical_not(ends[flow]))
                def _():
                    inbox[b] = part[b] + inbox[b]
                    reduce_copy(flow, q, inbox).start()

        for flow in range(2):
            p = t - (2 * (n_col - 1) - hops[flow]) * LAG

            @pl.when((p >= 0) & (p < count))
            def _():
                @pl.when(jnp.logical_not(ends[flow]))
                def _():
                    cast_copy(flow, p).wait_recv()

                    @pl.when(jnp.logical_not(starts[flow]))
                    def _():
                        cast_copy(flow, p).start()

                x = out[flow * count + p]
                grams[0] += dot_nt(x, x)

        return carry

    lax.fori_loop(0, count + 2 * (n_col - 1) * LAG, step, 0)
    for bit in range(bits):
        copy = pltpu.make_async_remote_copy(
            src_ref=grams.at[bit],
            dst_ref=gram_in.at[bit],
            send_sem=s_gram.at[bit],
            recv_sem=r_gram.at[bit],
            device_id={"row": partner_of(row, bit)},
            device_id_type=MESH,
        )
        copy.start()
        copy.wait()
        grams[bit + 1] = grams[bit] + gram_in[bit]
    gram[...] = grams[bits]

    def drain(q, carry):
        for flow in range(2):

            @pl.when(jnp.logical_not(ends[flow]))
            def _():
                reduce_copy(flow, q, part).wait_send()

            @pl.when(jnp.logical_not(starts[flow]))
            def _():
                cast_copy(flow, q).wait_send()

        return carry

    lax.fori_loop(0, count, drain, 0)


def line_call(n_col, bits, part):
    blocks = part.shape[0]
    dma = pltpu.SemaphoreType.DMA
    return pl.pallas_call(
        functools.partial(line_kernel, n_col, bits),
        out_shape=(
            jax.ShapeDtypeStruct(part.shape, jnp.float32),
            jax.ShapeDtypeStruct((K, K), jnp.float32),
        ),
        in_specs=[VMEM],
        out_specs=(VMEM, VMEM),
        scratch_shapes=[
            pltpu.VMEM(part.shape, jnp.float32),
            pltpu.VMEM((bits + 1, K, K), jnp.float32),
            pltpu.VMEM((bits, K, K), jnp.float32),
            dma((2, blocks // 2)),
            dma((2, blocks // 2)),
            dma((2, blocks // 2)),
            dma((2, blocks // 2)),
            dma((bits,)),
            dma((bits,)),
        ],
        compiler_params=pltpu.CompilerParams(
            collective_id=0, has_side_effects=True, vmem_limit_bytes=32 << 20
        ),
    )(part)


def halving_kernel(bits, scale, part, gram, out, inverse, *scratch):
    inboxes, s_sem, r_sem = scratch[:bits], scratch[bits], scratch[bits + 1]
    row = lax.axis_index("row")
    n_row = 1 << bits
    per = part.shape[0] // n_row
    kh = K // 2
    greet(0, bits)
    orders = (list(range(bits)), [0] + list(range(bits - 1, 0, -1)))

    def bit_of(index, bit):
        return (index // (1 << bit)) % 2

    def at(level, stream, mine, e):
        order = orders[stream]
        value = bit_of(row, order[level])
        value = value if mine else 1 - value
        rest = bits - 1 - level
        if level:
            return inboxes[level - 1].at[stream, value * (1 << rest) + e]
        dest = value * (1 << order[0])
        for i in range(rest):
            dest = dest + ((e >> (rest - 1 - i)) & 1) * (1 << order[1 + i])
        return part.at[pl.ds(dest * per, per), pl.ds(stream * kh, kh)]

    def copy_of(level, stream, e):
        base = sum(1 << (bits - 1 - l) for l in range(level))
        return pltpu.make_async_remote_copy(
            src_ref=at(level, stream, False, e),
            dst_ref=inboxes[level].at[stream, e],
            send_sem=s_sem.at[stream, base + e],
            recv_sem=r_sem.at[stream, base + e],
            device_id={"row": partner_of(row, orders[stream][level])},
            device_id_type=MESH,
        )

    panels = inverse_panels(scale, gram, inverse)
    sent = []
    for level in range(bits):
        slots = range(1 << (bits - 1 - level))
        copies = [(e, stream, copy_of(level, stream, e)) for e in slots for stream in range(2)]
        for _, _, copy in copies:
            copy.start()
        next(panels, None)
        for e, stream, copy in copies:
            copy.wait_recv()
            total = inboxes[level][stream, e] + at(level, stream, True, e)[...]
            if level < bits - 1:
                inboxes[level][stream, e] = total
            else:
                out[:, stream * kh : (stream + 1) * kh, :] = total
        sent += copies
    for _ in panels:
        pass
    for _, _, copy in sent:
        copy.wait_send()


def halving_call(bits, scale, part, gram):
    blocks, _, lanes = part.shape
    per = blocks >> bits
    dma = pltpu.SemaphoreType.DMA
    return pl.pallas_call(
        functools.partial(halving_kernel, bits, scale),
        out_shape=(
            jax.ShapeDtypeStruct((per, K, lanes), jnp.float32),
            jax.ShapeDtypeStruct((K, K), jnp.float32),
        ),
        in_specs=[VMEM, VMEM],
        out_specs=(VMEM, VMEM),
        scratch_shapes=[
            pltpu.VMEM((2, 1 << (bits - 1 - level), per, K // 2, lanes), jnp.float32)
            for level in range(bits)
        ]
        + [dma((2, (1 << bits) - 1)), dma((2, (1 << bits) - 1))],
        compiler_params=pltpu.CompilerParams(
            collective_id=1, has_side_effects=True, vmem_limit_bytes=32 << 20
        ),
    )(part, gram)


def dot_nt(a, b):
    return lax.dot_general(
        a, b, (((1,), (1,)), ((), ())), precision=HIGHEST, preferred_element_type=jnp.float32
    )


def invert_block(d):
    b = d.shape[0]
    rows = lax.broadcasted_iota(jnp.int32, (b, 1), 0)
    eye = (rows == lax.broadcasted_iota(jnp.int32, (b, b), 1)).astype(jnp.float32)
    x = jnp.concatenate([d, eye], axis=1)
    pivots = jnp.zeros((b, 1), jnp.float32)
    for k in range(b):
        row = x[k : k + 1, :]
        pivot = x[k : k + 1, k : k + 1]
        pivots = jnp.where(rows == k, pivot, pivots)
        ratio = jnp.where(rows > k, x[:, k : k + 1] / pivot, 0.0)
        x = x - ratio * row
    return x[:, b:] * lax.rsqrt(pivots)


def inverse_panels(scale, gram, out):
    b = K // 3
    g = gram[...]
    w = scale * (
        lax.broadcasted_iota(jnp.int32, (K, K), 0) == lax.broadcasted_iota(jnp.int32, (K, K), 1)
    ).astype(jnp.float32)
    for p in range(3):
        inverse = invert_block(g[:b, :b])
        top = jnp.dot(inverse, w[:b], precision=HIGHEST, preferred_element_type=jnp.float32)
        out[p * b : (p + 1) * b, :] = top
        if p < 2:
            lower = dot_nt(g[b:, :b], inverse)
            g = g[b:, b:] - dot_nt(lower, lower)
            w = w[b:] - jnp.dot(lower, top, precision=HIGHEST, preferred_element_type=jnp.float32)
        yield


def per_device(tile_values, tile_coords, live_counts):
    tb = tile_values.shape[1]
    col = lax.axis_index("col")
    n_col, n_row = lax.axis_size("col"), lax.axis_size("row")
    bits = n_row.bit_length() - 1
    base = (col * (CT * tb)).reshape(1)
    scale = math.sqrt(RT * tb * n_row)
    part = sketch_call(tile_coords, live_counts, base, tile_values)
    full, gram = line_call(n_col, bits, part)
    share_blocks = full.shape[0] // n_col
    share = lax.dynamic_slice_in_dim(full, col * share_blocks, share_blocks, 0)
    adjoint = adjoint_call(tile_coords, live_counts, tile_values, full)
    mine, inverse = halving_call(bits, scale, adjoint, gram)
    basis = jnp.einsum("bkn,lk->bnl", share, inverse, precision=HIGHEST).reshape(-1, K)
    projected = jnp.einsum("bkn,lk->bnl", mine, inverse, precision=HIGHEST).reshape(1, -1, K)
    return basis, projected


def solution(mesh):
    in_specs = (P(("row", "col"), None, None), P(("row", "col"), None), P(("row", "col")))
    out_specs = (P(("row", "col"), None), P("col", "row", None))
    return jax.shard_map(
        per_device, mesh=mesh, in_specs=in_specs, out_specs=out_specs, check_vma=False
    )
```

```python
import functools
import math

import jax
import jax.numpy as jnp
from jax import lax
from jax.experimental import pallas as pl
from jax.experimental.pallas import tpu as pltpu
from jax.sharding import PartitionSpec as P

K = 192
RT = 16
CT = 16
CHUNKS = 12
LAG = 2
HIGHEST = lax.Precision.HIGHEST


def load_tiles(tiles_hbm, tiles, sems):
    per = tiles.shape[0] // CHUNKS
    return [
        pltpu.make_async_copy(
            tiles_hbm.at[pl.ds(c * per, per)], tiles.at[pl.ds(c * per, per)], sems.at[c]
        )
        for c in range(CHUNKS)
    ]


def sketch_kernel(coords, live, base, tiles_hbm, out, tiles, signs, sems):
    tb = tiles.shape[1]
    half = tb // 2
    copies = load_tiles(tiles_hbm, tiles, sems)
    for copy in copies:
        copy.start()
    out[...] = jnp.zeros_like(out)

    def make_signs(j, carry):
        column = lax.broadcasted_iota(jnp.int32, (K, tb), 1) + (base[0] + j * tb)
        h = column * K + lax.broadcasted_iota(jnp.int32, (K, tb), 0)
        h = h * 747796405 + 1442695040
        h = h ^ (h >> 15)
        h = h * 1103515245 + 12345
        h = h ^ (h >> 13)
        signs[j] = (1 - 2 * ((h >> 9) & 1)).astype(jnp.float32).astype(jnp.bfloat16)
        return carry

    lax.fori_loop(0, CT, make_signs, 0)
    per = tiles.shape[0] // CHUNKS
    for c, copy in enumerate(copies):
        copy.wait()

        def step(s, carry):
            i = coords[s, 0]
            j = coords[s, 1]
            t = lax.dot_general(
                signs[j], tiles[s], (((1,), (1,)), ((), ())), preferred_element_type=jnp.float32
            )
            out[2 * i] += t[:, :half]
            out[2 * i + 1] += t[:, half:]
            return carry

        lax.fori_loop(c * per, jnp.minimum((c + 1) * per, live[0]), step, 0)


def adjoint_kernel(coords, live, tiles_hbm, parts_hbm, out, tiles, parts, sems, parts_sem):
    half = out.shape[2]
    parts_copy = pltpu.make_async_copy(parts_hbm, parts, parts_sem)
    parts_copy.start()
    copies = load_tiles(tiles_hbm, tiles, sems)
    for copy in copies:
        copy.start()
    out[...] = jnp.zeros_like(out)
    parts_copy.wait()
    per = tiles.shape[0] // CHUNKS
    for c, copy in enumerate(copies):
        copy.wait()

        def step(s, carry):
            i = coords[s, 0]
            j = coords[s, 1]
            t = jnp.dot(parts[i], tiles[s], preferred_element_type=jnp.float32)
            t = t[:K] + t[K : 2 * K] + t[2 * K :]
            out[2 * j] += t[:, :half]
            out[2 * j + 1] += t[:, half:]
            return carry

        lax.fori_loop(c * per, jnp.minimum((c + 1) * per, live[0]), step, 0)


MESH = pl.DeviceIdType.MESH
SMEM = pl.BlockSpec(memory_space=pltpu.SMEM)
VMEM = pl.BlockSpec(memory_space=pltpu.VMEM)
ANY = pl.BlockSpec(memory_space=pl.ANY)


def sketch_call(tile_coords, live_counts, base, tile_values):
    slots, tb, _ = tile_values.shape
    return pl.pallas_call(
        sketch_kernel,
        out_shape=jax.ShapeDtypeStruct((2 * RT, K, tb // 2), jnp.float32),
        in_specs=[SMEM, SMEM, SMEM, ANY],
        out_specs=VMEM,
        scratch_shapes=[
            pltpu.VMEM((slots, tb, tb), jnp.bfloat16),
            pltpu.VMEM((CT, K, tb), jnp.bfloat16),
            pltpu.SemaphoreType.DMA((CHUNKS,)),
        ],
        compiler_params=pltpu.CompilerParams(vmem_limit_bytes=40 << 20),
        cost_estimate=pl.CostEstimate(
            flops=2 * slots * tb * tb * K, bytes_accessed=slots * tb * tb * 2, transcendentals=0
        ),
    )(tile_coords, live_counts, base, tile_values)


def adjoint_call(tile_coords, live_counts, tile_values, parts):
    slots, tb, _ = tile_values.shape
    return pl.pallas_call(
        adjoint_kernel,
        out_shape=jax.ShapeDtypeStruct((2 * CT, K, tb // 2), jnp.float32),
        in_specs=[SMEM, SMEM, ANY, ANY],
        out_specs=VMEM,
        scratch_shapes=[
            pltpu.VMEM((slots, tb, tb), jnp.bfloat16),
            pltpu.VMEM(parts.shape, jnp.bfloat16),
            pltpu.SemaphoreType.DMA((CHUNKS,)),
            pltpu.SemaphoreType.DMA,
        ],
        compiler_params=pltpu.CompilerParams(vmem_limit_bytes=48 << 20),
        cost_estimate=pl.CostEstimate(
            flops=6 * slots * tb * tb * K, bytes_accessed=slots * tb * tb * 2, transcendentals=0
        ),
    )(tile_coords, live_counts, tile_values, parts)


def partner_of(index, bit):
    step = 1 << bit
    return index + step * (1 - 2 * ((index // step) % 2))


def greet(n_col, bits):
    barrier = pltpu.get_barrier_semaphore()
    col = lax.axis_index("col")
    row = lax.axis_index("row")
    expected = bits
    for bit in range(bits):
        pl.semaphore_signal(barrier, inc=1, device_id={"row": partner_of(row, bit)}, device_id_type=MESH)
    if n_col:

        @pl.when(col > 0)
        def _():
            pl.semaphore_signal(barrier, inc=1, device_id={"col": col - 1}, device_id_type=MESH)

        @pl.when(col < n_col - 1)
        def _():
            pl.semaphore_signal(barrier, inc=1, device_id={"col": col + 1}, device_id_type=MESH)

        expected = bits + jnp.where(col > 0, 1, 0) + jnp.where(col < n_col - 1, 1, 0)
    pl.semaphore_wait(barrier, expected)


def line_kernel(
    n_col,
    bits,
    part,
    out,
    parts,
    gram,
    inbox,
    products,
    squares,
    halves,
    grams,
    gram_in,
    s_red,
    r_red,
    s_cast,
    r_cast,
    s_gram,
    r_gram,
):
    col = lax.axis_index("col")
    row = lax.axis_index("row")
    count = part.shape[0] // 2
    greet(n_col, bits)
    first = (col == 0, col == n_col - 1)
    ends = (first[0], first[1])
    starts = (first[1], first[0])
    towards = (col - 1, col + 1)
    away = (col + 1, col - 1)

    def reduce_copy(flow, q, src):
        return pltpu.make_async_remote_copy(
            src_ref=src.at[flow * count + q],
            dst_ref=inbox.at[flow * count + q],
            send_sem=s_red.at[flow, q],
            recv_sem=r_red.at[flow, q],
            device_id={"col": towards[flow]},
            device_id_type=MESH,
        )

    def cast_copy(flow, q):
        return pltpu.make_async_remote_copy(
            src_ref=out.at[flow * count + q],
            dst_ref=out.at[flow * count + q],
            send_sem=s_cast.at[flow, q],
            recv_sem=r_cast.at[flow, q],
            device_id={"col": away[flow]},
            device_id_type=MESH,
        )

    for flow in range(2):

        @pl.when(starts[flow])
        def _():
            def send(q, carry):
                reduce_copy(flow, q, part).start()
                return carry

            lax.fori_loop(0, count, send, 0)

    products[...] = jnp.zeros_like(products)
    squares[...] = jnp.zeros_like(squares)
    hops = (n_col - 1 - col, col)

    def step(t, carry):
        for flow in range(2):
            q = t - hops[flow] * LAG
            b = flow * count + q

            @pl.when((q >= 0) & (q < count) & jnp.logical_not(starts[flow]))
            def _():
                reduce_copy(flow, q, part).wait_recv()

                @pl.when(ends[flow])
                def _():
                    out[b] = part[b] + inbox[b]
                    cast_copy(flow, q).start()

                @pl.when(jnp.logical_not(ends[flow]))
                def _():
                    inbox[b] = part[b] + inbox[b]
                    reduce_copy(flow, q, inbox).start()

        for flow in range(2):
            p = t - (2 * (n_col - 1) - hops[flow]) * LAG

            @pl.when((p >= 0) & (p < count))
            def _():
                @pl.when(jnp.logical_not(ends[flow]))
                def _():
                    cast_copy(flow, p).wait_recv()

                    @pl.when(jnp.logical_not(starts[flow]))
                    def _():
                        cast_copy(flow, p).start()

                @pl.when(p % 2 == 1)
                def _():
                    b = flow * count + p
                    x = jnp.concatenate([out[b - 1], out[b]], axis=1)
                    high = x.astype(jnp.bfloat16)
                    x = x - high.astype(jnp.float32)
                    middle = x.astype(jnp.bfloat16)
                    low = (x - middle.astype(jnp.float32)).astype(jnp.bfloat16)
                    terms = jnp.concatenate([high, middle, low], axis=0)
                    parts[b // 2] = terms
                    products[...] += narrow_nt(terms, high)
                    squares[...] += narrow_nt(middle, middle)

        return carry

    lax.fori_loop(0, count + 2 * (n_col - 1) * LAG, step, 0)
    cross = products[K : 2 * K] + products[2 * K :]
    total = products[:K] + squares[...] + cross + cross.T
    halves[0] = total[: K // 2]
    halves[1] = total[K // 2 :]
    core = row % 2

    def gram_copy(step, src, dst, bit):
        return pltpu.make_async_remote_copy(
            src_ref=src,
            dst_ref=dst,
            send_sem=s_gram.at[step],
            recv_sem=r_gram.at[step],
            device_id={"row": partner_of(row, bit)},
            device_id_type=MESH,
        )

    for bit in range(bits):
        src = grams.at[bit - 1] if bit else halves.at[1 - core]
        copy = gram_copy(bit, src, gram_in.at[bit], bit)
        copy.start()
        copy.wait()
        grams[bit] = (grams[bit - 1] if bit else halves[core]) + gram_in[bit]
    copy = gram_copy(bits, grams.at[bits - 1], gram_in.at[bits], 0)
    copy.start()
    copy.wait()
    gram[pl.ds(pl.multiple_of(core * (K // 2), 8), K // 2), :] = grams[bits - 1]
    gram[pl.ds(pl.multiple_of((1 - core) * (K // 2), 8), K // 2), :] = gram_in[bits]

    def drain(q, carry):
        for flow in range(2):

            @pl.when(jnp.logical_not(ends[flow]))
            def _():
                reduce_copy(flow, q, part).wait_send()

            @pl.when(jnp.logical_not(starts[flow]))
            def _():
                cast_copy(flow, q).wait_send()

        return carry

    lax.fori_loop(0, count, drain, 0)


def line_call(n_col, bits, part):
    blocks = part.shape[0]
    dma = pltpu.SemaphoreType.DMA
    return pl.pallas_call(
        functools.partial(line_kernel, n_col, bits),
        out_shape=(
            jax.ShapeDtypeStruct(part.shape, jnp.float32),
            jax.ShapeDtypeStruct((RT, 3 * K, 2 * part.shape[2]), jnp.bfloat16),
            jax.ShapeDtypeStruct((K, K), jnp.float32),
        ),
        in_specs=[VMEM],
        out_specs=(VMEM, VMEM, VMEM),
        scratch_shapes=[
            pltpu.VMEM(part.shape, jnp.float32),
            pltpu.VMEM((3 * K, K), jnp.float32),
            pltpu.VMEM((K, K), jnp.float32),
            pltpu.VMEM((2, K // 2, K), jnp.float32),
            pltpu.VMEM((bits, K // 2, K), jnp.float32),
            pltpu.VMEM((bits + 1, K // 2, K), jnp.float32),
            dma((2, blocks // 2)),
            dma((2, blocks // 2)),
            dma((2, blocks // 2)),
            dma((2, blocks // 2)),
            dma((bits + 1,)),
            dma((bits + 1,)),
        ],
        compiler_params=pltpu.CompilerParams(
            collective_id=0, has_side_effects=True, vmem_limit_bytes=32 << 20
        ),
    )(part)


def halving_kernel(bits, scale, part, gram, out, inverse, *scratch):
    inboxes, s_sem, r_sem = scratch[:bits], scratch[bits], scratch[bits + 1]
    row = lax.axis_index("row")
    n_row = 1 << bits
    per = part.shape[0] // n_row
    kh = K // 2
    greet(0, bits)
    orders = (list(range(bits)), [0] + list(range(bits - 1, 0, -1)))

    def bit_of(index, bit):
        return (index // (1 << bit)) % 2

    def at(level, stream, mine, e):
        order = orders[stream]
        value = bit_of(row, order[level])
        value = value if mine else 1 - value
        rest = bits - 1 - level
        if level:
            return inboxes[level - 1].at[stream, value * (1 << rest) + e]
        dest = value * (1 << order[0])
        for i in range(rest):
            dest = dest + ((e >> (rest - 1 - i)) & 1) * (1 << order[1 + i])
        return part.at[pl.ds(dest * per, per), pl.ds(stream * kh, kh)]

    def copy_of(level, stream, e):
        base = sum(1 << (bits - 1 - l) for l in range(level))
        return pltpu.make_async_remote_copy(
            src_ref=at(level, stream, False, e),
            dst_ref=inboxes[level].at[stream, e],
            send_sem=s_sem.at[stream, base + e],
            recv_sem=r_sem.at[stream, base + e],
            device_id={"row": partner_of(row, orders[stream][level])},
            device_id_type=MESH,
        )

    panels = inverse_panels(scale, gram, inverse)
    sent = []
    for level in range(bits):
        slots = range(1 << (bits - 1 - level))
        copies = [(e, stream, copy_of(level, stream, e)) for e in slots for stream in range(2)]
        for _, _, copy in copies:
            copy.start()
        next(panels, None)
        for e, stream, copy in copies:
            copy.wait_recv()
            total = inboxes[level][stream, e] + at(level, stream, True, e)[...]
            if level < bits - 1:
                inboxes[level][stream, e] = total
            else:
                out[:, stream * kh : (stream + 1) * kh, :] = total
        sent += copies
    for _ in panels:
        pass
    for _, _, copy in sent:
        copy.wait_send()


def halving_call(bits, scale, part, gram):
    blocks, _, lanes = part.shape
    per = blocks >> bits
    dma = pltpu.SemaphoreType.DMA
    return pl.pallas_call(
        functools.partial(halving_kernel, bits, scale),
        out_shape=(
            jax.ShapeDtypeStruct((per, K, lanes), jnp.float32),
            jax.ShapeDtypeStruct((K, K), jnp.float32),
        ),
        in_specs=[VMEM, VMEM],
        out_specs=(VMEM, VMEM),
        scratch_shapes=[
            pltpu.VMEM((2, 1 << (bits - 1 - level), per, K // 2, lanes), jnp.float32)
            for level in range(bits)
        ]
        + [dma((2, (1 << bits) - 1)), dma((2, (1 << bits) - 1))],
        compiler_params=pltpu.CompilerParams(
            collective_id=1, has_side_effects=True, vmem_limit_bytes=32 << 20
        ),
    )(part, gram)


def narrow_nt(a, b):
    return lax.dot_general(a, b, (((1,), (1,)), ((), ())), preferred_element_type=jnp.float32)


def dot_nt(a, b):
    return lax.dot_general(
        a, b, (((1,), (1,)), ((), ())), precision=HIGHEST, preferred_element_type=jnp.float32
    )


def invert_block(d):
    b = d.shape[0]
    rows = lax.broadcasted_iota(jnp.int32, (b, 1), 0)
    eye = (rows == lax.broadcasted_iota(jnp.int32, (b, b), 1)).astype(jnp.float32)
    x = jnp.concatenate([d, eye], axis=1)
    pivots = jnp.ones_like(x)
    for start in range(0, b, 4):
        columns = [jnp.broadcast_to(x[:, k : k + 1], x.shape) for k in range(start, start + 4)]
        for i in range(4):
            k = start + i
            pivot = columns[i][k : k + 1, :]
            pivots = jnp.where(rows == k, pivot, pivots)
            ratio = jnp.where(rows > k, columns[i] * (1.0 / pivot), 0.0)
            for j in range(i + 1, 4):
                columns[j] = columns[j] - ratio * columns[j][k : k + 1, :]
            x = x - ratio * x[k : k + 1, :]
    return x[:, b:] * lax.rsqrt(pivots)[:, b:]


def inverse_panels(scale, gram, out):
    b = K // 3
    g = gram[...]
    w = scale * (
        lax.broadcasted_iota(jnp.int32, (K, K), 0) == lax.broadcasted_iota(jnp.int32, (K, K), 1)
    ).astype(jnp.float32)
    for p in range(3):
        inverse = invert_block(g[:b, :b])
        top = jnp.dot(inverse, w[:b], precision=HIGHEST, preferred_element_type=jnp.float32)
        out[p * b : (p + 1) * b, :] = top
        if p < 2:
            lower = dot_nt(g[b:, :b], inverse)
            g = g[b:, b:] - dot_nt(lower, lower)
            w = w[b:] - jnp.dot(lower, top, precision=HIGHEST, preferred_element_type=jnp.float32)
        yield


def per_device(tile_values, tile_coords, live_counts):
    tb = tile_values.shape[1]
    col = lax.axis_index("col")
    n_col, n_row = lax.axis_size("col"), lax.axis_size("row")
    bits = n_row.bit_length() - 1
    base = (col * (CT * tb)).reshape(1)
    scale = math.sqrt(RT * tb * n_row)
    part = sketch_call(tile_coords, live_counts, base, tile_values)
    full, parts, gram = line_call(n_col, bits, part)
    share_blocks = full.shape[0] // n_col
    share = lax.dynamic_slice_in_dim(full, col * share_blocks, share_blocks, 0)
    adjoint = adjoint_call(tile_coords, live_counts, tile_values, parts)
    mine, inverse = halving_call(bits, scale, adjoint, gram)
    basis = jnp.einsum("bkn,lk->bnl", share, inverse, precision=HIGHEST).reshape(-1, K)
    projected = jnp.einsum("bkn,lk->bnl", mine, inverse, precision=HIGHEST).reshape(1, -1, K)
    return basis, projected


def solution(mesh):
    in_specs = (P(("row", "col"), None, None), P(("row", "col"), None), P(("row", "col")))
    out_specs = (P(("row", "col"), None), P("col", "row", None))
    return jax.shard_map(
        per_device, mesh=mesh, in_specs=in_specs, out_specs=out_specs, check_vma=False
    )
```

```python
import functools
import math

import jax
import jax.numpy as jnp
from jax import lax
from jax.experimental import pallas as pl
from jax.experimental.pallas import tpu as pltpu
from jax.sharding import PartitionSpec as P

K = 192
RT = 16
CT = 16
CHUNKS = 12
LAG = 3
HIGHEST = lax.Precision.HIGHEST


def load_tiles(tiles_hbm, tiles, sems):
    per = tiles.shape[0] // CHUNKS
    return [
        pltpu.make_async_copy(
            tiles_hbm.at[pl.ds(c * per, per)], tiles.at[pl.ds(c * per, per)], sems.at[c]
        )
        for c in range(CHUNKS)
    ]


def sketch_kernel(coords, live, base, tiles_hbm, out, tiles, signs, sems):
    tb = tiles.shape[1]
    half = tb // 2
    copies = load_tiles(tiles_hbm, tiles, sems)
    for copy in copies:
        copy.start()
    out[...] = jnp.zeros_like(out)

    def make_signs(j, carry):
        column = lax.broadcasted_iota(jnp.int32, (K, tb), 1) + (base[0] + j * tb)
        h = column * K + lax.broadcasted_iota(jnp.int32, (K, tb), 0)
        h = h * 747796405 + 1442695040
        h = h ^ (h >> 15)
        h = h * 1103515245 + 12345
        h = h ^ (h >> 13)
        signs[j] = (1 - 2 * ((h >> 9) & 1)).astype(jnp.float32).astype(jnp.bfloat16)
        return carry

    lax.fori_loop(0, CT, make_signs, 0)
    per = tiles.shape[0] // CHUNKS
    for c, copy in enumerate(copies):
        copy.wait()

        def step(group, carry):
            terms = []
            for s in range(4):
                s = group * 4 + s
                t = lax.dot_general(
                    signs[coords[s, 1]],
                    tiles[s],
                    (((1,), (1,)), ((), ())),
                    preferred_element_type=jnp.float32,
                )
                terms.append((coords[s, 0], jnp.where(s < live[0], t, 0.0)))
            for i, t in terms:
                out[2 * i] += t[:, :half]
                out[2 * i + 1] += t[:, half:]
            return carry

        lax.fori_loop(c * per // 4, jnp.minimum((c + 1) * per, live[0] + 3) // 4, step, 0)


def adjoint_kernel(coords, live, tiles_hbm, parts_hbm, out, tiles, parts, sems, parts_sem):
    half = out.shape[2]
    parts_copy = pltpu.make_async_copy(parts_hbm, parts, parts_sem)
    parts_copy.start()
    copies = load_tiles(tiles_hbm, tiles, sems)
    for copy in copies:
        copy.start()
    out[...] = jnp.zeros_like(out)
    parts_copy.wait()
    per = tiles.shape[0] // CHUNKS
    for c, copy in enumerate(copies):
        copy.wait()

        def step(group, carry):
            terms = []
            for s in range(4):
                s = group * 4 + s
                t = jnp.dot(parts[coords[s, 0]], tiles[s], preferred_element_type=jnp.float32)
                t = t[:K] + t[K : 2 * K] + t[2 * K :]
                terms.append((coords[s, 1], jnp.where(s < live[0], t, 0.0)))
            for j, t in terms:
                out[2 * j] += t[:, :half]
                out[2 * j + 1] += t[:, half:]
            return carry

        lax.fori_loop(c * per // 4, jnp.minimum((c + 1) * per, live[0] + 3) // 4, step, 0)


MESH = pl.DeviceIdType.MESH
SMEM = pl.BlockSpec(memory_space=pltpu.SMEM)
VMEM = pl.BlockSpec(memory_space=pltpu.VMEM)
ANY = pl.BlockSpec(memory_space=pl.ANY)


def sketch_call(tile_coords, live_counts, base, tile_values):
    slots, tb, _ = tile_values.shape
    return pl.pallas_call(
        sketch_kernel,
        out_shape=jax.ShapeDtypeStruct((2 * RT, K, tb // 2), jnp.float32),
        in_specs=[SMEM, SMEM, SMEM, ANY],
        out_specs=VMEM,
        scratch_shapes=[
            pltpu.VMEM((slots, tb, tb), jnp.bfloat16),
            pltpu.VMEM((CT, K, tb), jnp.bfloat16),
            pltpu.SemaphoreType.DMA((CHUNKS,)),
        ],
        compiler_params=pltpu.CompilerParams(vmem_limit_bytes=40 << 20),
        cost_estimate=pl.CostEstimate(
            flops=2 * slots * tb * tb * K, bytes_accessed=slots * tb * tb * 2, transcendentals=0
        ),
    )(tile_coords, live_counts, base, tile_values)


def adjoint_call(tile_coords, live_counts, tile_values, parts):
    slots, tb, _ = tile_values.shape
    return pl.pallas_call(
        adjoint_kernel,
        out_shape=jax.ShapeDtypeStruct((2 * CT, K, tb // 2), jnp.float32),
        in_specs=[SMEM, SMEM, ANY, ANY],
        out_specs=VMEM,
        scratch_shapes=[
            pltpu.VMEM((slots, tb, tb), jnp.bfloat16),
            pltpu.VMEM(parts.shape, jnp.bfloat16),
            pltpu.SemaphoreType.DMA((CHUNKS,)),
            pltpu.SemaphoreType.DMA,
        ],
        compiler_params=pltpu.CompilerParams(vmem_limit_bytes=48 << 20),
        cost_estimate=pl.CostEstimate(
            flops=6 * slots * tb * tb * K, bytes_accessed=slots * tb * tb * 2, transcendentals=0
        ),
    )(tile_coords, live_counts, tile_values, parts)


def partner_of(index, bit):
    step = 1 << bit
    return index + step * (1 - 2 * ((index // step) % 2))


def greet(n_col, bits):
    barrier = pltpu.get_barrier_semaphore()
    col = lax.axis_index("col")
    row = lax.axis_index("row")
    expected = bits
    for bit in range(bits):
        pl.semaphore_signal(barrier, inc=1, device_id={"row": partner_of(row, bit)}, device_id_type=MESH)
    if n_col:

        @pl.when(col > 0)
        def _():
            pl.semaphore_signal(barrier, inc=1, device_id={"col": col - 1}, device_id_type=MESH)

        @pl.when(col < n_col - 1)
        def _():
            pl.semaphore_signal(barrier, inc=1, device_id={"col": col + 1}, device_id_type=MESH)

        expected = bits + jnp.where(col > 0, 1, 0) + jnp.where(col < n_col - 1, 1, 0)
    pl.semaphore_wait(barrier, expected)


def line_kernel(
    n_col,
    bits,
    part,
    share,
    parts,
    gram,
    out,
    inbox,
    products,
    squares,
    halves,
    grams,
    gram_in,
    s_red,
    r_red,
    s_cast,
    r_cast,
    s_gram,
    r_gram,
):
    col = lax.axis_index("col")
    row = lax.axis_index("row")
    count = part.shape[0] // 2
    greet(n_col, bits)
    first = (col == 0, col == n_col - 1)
    ends = (first[0], first[1])
    starts = (first[1], first[0])
    towards = (col - 1, col + 1)
    away = (col + 1, col - 1)

    def reduce_copy(flow, q, src):
        return pltpu.make_async_remote_copy(
            src_ref=src.at[flow * count + q],
            dst_ref=inbox.at[flow * count + q],
            send_sem=s_red.at[flow, q],
            recv_sem=r_red.at[flow, q],
            device_id={"col": towards[flow]},
            device_id_type=MESH,
        )

    def cast_copy(flow, q):
        return pltpu.make_async_remote_copy(
            src_ref=out.at[flow * count + q],
            dst_ref=out.at[flow * count + q],
            send_sem=s_cast.at[flow, q],
            recv_sem=r_cast.at[flow, q],
            device_id={"col": away[flow]},
            device_id_type=MESH,
        )

    for flow in range(2):

        @pl.when(starts[flow])
        def _():
            def send(q, carry):
                reduce_copy(flow, q, part).start()
                return carry

            lax.fori_loop(0, count, send, 0)

    products[...] = jnp.zeros_like(products)
    squares[...] = jnp.zeros_like(squares)
    hops = (n_col - 1 - col, col)

    def step(t, carry):
        for flow in range(2):
            q = t - hops[flow] * LAG
            b = flow * count + q

            @pl.when((q >= 0) & (q < count) & jnp.logical_not(starts[flow]))
            def _():
                reduce_copy(flow, q, part).wait_recv()

                @pl.when(ends[flow])
                def _():
                    out[b] = part[b] + inbox[b]
                    cast_copy(flow, q).start()

                @pl.when(jnp.logical_not(ends[flow]))
                def _():
                    inbox[b] = part[b] + inbox[b]
                    reduce_copy(flow, q, inbox).start()

        for flow in range(2):
            p = t - (2 * (n_col - 1) - hops[flow]) * LAG

            @pl.when((p >= 0) & (p < count))
            def _():
                @pl.when(jnp.logical_not(ends[flow]))
                def _():
                    cast_copy(flow, p).wait_recv()

                    @pl.when(jnp.logical_not(starts[flow]))
                    def _():
                        cast_copy(flow, p).start()

                @pl.when(p % 4 == 3)
                def _():
                    b = flow * count + p
                    left = jnp.concatenate([out[b - 3], out[b - 2]], axis=0)
                    right = jnp.concatenate([out[b - 1], out[b]], axis=0)
                    x = jnp.concatenate([left, right], axis=1)
                    high = x.astype(jnp.bfloat16)
                    x = x - high.astype(jnp.float32)
                    middle = x.astype(jnp.bfloat16)
                    low = (x - middle.astype(jnp.float32)).astype(jnp.bfloat16)
                    terms = jnp.concatenate([high, middle, low], axis=0)
                    parts[b // 4] = terms
                    products[...] += narrow_nt(terms, high)
                    squares[...] += narrow_nt(middle, middle)

        return carry

    lax.fori_loop(0, count + 2 * (n_col - 1) * LAG, step, 0)
    cross = products[K : 2 * K] + products[2 * K :]
    total = products[:K] + squares[...] + cross + cross.T
    halves[0] = total[: K // 2]
    halves[1] = total[K // 2 :]
    core = row % 2

    def gram_copy(step, src, dst, bit):
        return pltpu.make_async_remote_copy(
            src_ref=src,
            dst_ref=dst,
            send_sem=s_gram.at[step],
            recv_sem=r_gram.at[step],
            device_id={"row": partner_of(row, bit)},
            device_id_type=MESH,
        )

    for bit in range(bits):
        src = grams.at[bit - 1] if bit else halves.at[1 - core]
        copy = gram_copy(bit, src, gram_in.at[bit], bit)
        copy.start()
        copy.wait()
        grams[bit] = (grams[bit - 1] if bit else halves[core]) + gram_in[bit]
    copy = gram_copy(bits, grams.at[bits - 1], gram_in.at[bits], 0)
    copy.start()
    copy.wait()
    gram[pl.ds(pl.multiple_of(core * (K // 2), 8), K // 2), :] = grams[bits - 1]
    gram[pl.ds(pl.multiple_of((1 - core) * (K // 2), 8), K // 2), :] = gram_in[bits]

    own = share.shape[0]
    share[...] = out[pl.ds(col * own, own)]

    def drain(q, carry):
        for flow in range(2):

            @pl.when(jnp.logical_not(ends[flow]))
            def _():
                reduce_copy(flow, q, part).wait_send()

            @pl.when(jnp.logical_not(starts[flow]))
            def _():
                cast_copy(flow, q).wait_send()

        return carry

    lax.fori_loop(0, count, drain, 0)


def line_call(n_col, bits, part):
    blocks = part.shape[0]
    dma = pltpu.SemaphoreType.DMA
    return pl.pallas_call(
        functools.partial(line_kernel, n_col, bits),
        out_shape=(
            jax.ShapeDtypeStruct((blocks // n_col,) + part.shape[1:], jnp.float32),
            jax.ShapeDtypeStruct((RT, 3 * K, 2 * part.shape[2]), jnp.bfloat16),
            jax.ShapeDtypeStruct((K, K), jnp.float32),
        ),
        in_specs=[VMEM],
        out_specs=(VMEM, VMEM, VMEM),
        scratch_shapes=[
            pltpu.VMEM(part.shape, jnp.float32),
            pltpu.VMEM(part.shape, jnp.float32),
            pltpu.VMEM((3 * K, K), jnp.float32),
            pltpu.VMEM((K, K), jnp.float32),
            pltpu.VMEM((2, K // 2, K), jnp.float32),
            pltpu.VMEM((bits, K // 2, K), jnp.float32),
            pltpu.VMEM((bits + 1, K // 2, K), jnp.float32),
            dma((2, blocks // 2)),
            dma((2, blocks // 2)),
            dma((2, blocks // 2)),
            dma((2, blocks // 2)),
            dma((bits + 1,)),
            dma((bits + 1,)),
        ],
        compiler_params=pltpu.CompilerParams(
            collective_id=0, has_side_effects=True, vmem_limit_bytes=32 << 20
        ),
    )(part)


def halving_kernel(bits, scale, part, gram, out, inverse, *scratch):
    inboxes, s_sem, r_sem = scratch[:bits], scratch[bits], scratch[bits + 1]
    row = lax.axis_index("row")
    n_row = 1 << bits
    per = part.shape[0] // n_row
    kh = K // 2
    greet(0, bits)
    orders = (list(range(bits)), [0] + list(range(bits - 1, 0, -1)))

    def bit_of(index, bit):
        return (index // (1 << bit)) % 2

    def at(level, stream, mine, e):
        order = orders[stream]
        value = bit_of(row, order[level])
        value = value if mine else 1 - value
        rest = bits - 1 - level
        if level:
            return inboxes[level - 1].at[stream, value * (1 << rest) + e]
        dest = value * (1 << order[0])
        for i in range(rest):
            dest = dest + ((e >> (rest - 1 - i)) & 1) * (1 << order[1 + i])
        return part.at[pl.ds(dest * per, per), pl.ds(stream * kh, kh)]

    def copy_of(level, stream, e):
        base = sum(1 << (bits - 1 - l) for l in range(level))
        return pltpu.make_async_remote_copy(
            src_ref=at(level, stream, False, e),
            dst_ref=inboxes[level].at[stream, e],
            send_sem=s_sem.at[stream, base + e],
            recv_sem=r_sem.at[stream, base + e],
            device_id={"row": partner_of(row, orders[stream][level])},
            device_id_type=MESH,
        )

    panels = inverse_panels(scale, gram, inverse)
    sent = []
    for level in range(bits):
        slots = range(1 << (bits - 1 - level))
        copies = [(e, stream, copy_of(level, stream, e)) for e in slots for stream in range(2)]
        for _, _, copy in copies:
            copy.start()
        next(panels, None)
        for e, stream, copy in copies:
            copy.wait_recv()
            total = inboxes[level][stream, e] + at(level, stream, True, e)[...]
            if level < bits - 1:
                inboxes[level][stream, e] = total
            else:
                out[:, stream * kh : (stream + 1) * kh, :] = total
        sent += copies
    for _ in panels:
        pass
    for _, _, copy in sent:
        copy.wait_send()


def halving_call(bits, scale, part, gram):
    blocks, _, lanes = part.shape
    per = blocks >> bits
    dma = pltpu.SemaphoreType.DMA
    return pl.pallas_call(
        functools.partial(halving_kernel, bits, scale),
        out_shape=(
            jax.ShapeDtypeStruct((per, K, lanes), jnp.float32),
            jax.ShapeDtypeStruct((K, K), jnp.float32),
        ),
        in_specs=[VMEM, VMEM],
        out_specs=(VMEM, VMEM),
        scratch_shapes=[
            pltpu.VMEM((2, 1 << (bits - 1 - level), per, K // 2, lanes), jnp.float32)
            for level in range(bits)
        ]
        + [dma((2, (1 << bits) - 1)), dma((2, (1 << bits) - 1))],
        compiler_params=pltpu.CompilerParams(
            collective_id=1, has_side_effects=True, vmem_limit_bytes=32 << 20
        ),
    )(part, gram)


def narrow_nt(a, b):
    return lax.dot_general(a, b, (((1,), (1,)), ((), ())), preferred_element_type=jnp.float32)


def dot_nt(a, b):
    return lax.dot_general(
        a, b, (((1,), (1,)), ((), ())), precision=HIGHEST, preferred_element_type=jnp.float32
    )


def invert_block(d):
    b = d.shape[0]
    rows = lax.broadcasted_iota(jnp.int32, (b, 1), 0)
    eye = (rows == lax.broadcasted_iota(jnp.int32, (b, b), 1)).astype(jnp.float32)
    x = jnp.concatenate([d, eye], axis=1)
    pivots = jnp.ones_like(x)
    for start in range(0, b, 4):
        columns = [jnp.broadcast_to(x[:, k : k + 1], x.shape) for k in range(start, start + 4)]
        for i in range(4):
            k = start + i
            pivot = columns[i][k : k + 1, :]
            pivots = jnp.where(rows == k, pivot, pivots)
            ratio = jnp.where(rows > k, columns[i] * (1.0 / pivot), 0.0)
            for j in range(i + 1, 4):
                columns[j] = columns[j] - ratio * columns[j][k : k + 1, :]
            x = x - ratio * x[k : k + 1, :]
    return x[:, b:] * lax.rsqrt(pivots)[:, b:]


def inverse_panels(scale, gram, out):
    b = K // 3
    g = gram[...]
    w = scale * (
        lax.broadcasted_iota(jnp.int32, (K, K), 0) == lax.broadcasted_iota(jnp.int32, (K, K), 1)
    ).astype(jnp.float32)
    for p in range(3):
        inverse = invert_block(g[:b, :b])
        top = jnp.dot(inverse, w[:b], precision=HIGHEST, preferred_element_type=jnp.float32)
        out[p * b : (p + 1) * b, :] = top
        if p < 2:
            lower = dot_nt(g[b:, :b], inverse)
            g = g[b:, b:] - dot_nt(lower, lower)
            w = w[b:] - jnp.dot(lower, top, precision=HIGHEST, preferred_element_type=jnp.float32)
        yield


def per_device(tile_values, tile_coords, live_counts):
    tb = tile_values.shape[1]
    col = lax.axis_index("col")
    n_col, n_row = lax.axis_size("col"), lax.axis_size("row")
    bits = n_row.bit_length() - 1
    base = (col * (CT * tb)).reshape(1)
    scale = math.sqrt(RT * tb * n_row)
    part = sketch_call(tile_coords, live_counts, base, tile_values)
    lanes = part.shape[2]
    share, parts, gram = line_call(n_col, bits, part.reshape(-1, K // 2, lanes))
    share = share.reshape(-1, K, lanes)
    adjoint = adjoint_call(tile_coords, live_counts, tile_values, parts)
    mine, inverse = halving_call(bits, scale, adjoint, gram)
    basis = jnp.einsum("bkn,lk->bnl", share, inverse, precision=HIGHEST).reshape(-1, K)
    projected = jnp.einsum("bkn,lk->bnl", mine, inverse, precision=HIGHEST).reshape(1, -1, K)
    return basis, projected


def solution(mesh):
    in_specs = (P(("row", "col"), None, None), P(("row", "col"), None), P(("row", "col")))
    out_specs = (P(("row", "col"), None), P("col", "row", None))
    return jax.shard_map(
        per_device, mesh=mesh, in_specs=in_specs, out_specs=out_specs, check_vma=False
    )
```
